32 devices in a mesh: aux: 8 (over y, x, core), vir: 4 (over z).
Axes of the slice: x: 2, y: 2, z: 4, core: 2. Of those that a mesh axis runs over, the one named last changes fastest.
Arguments:
- integrals: float32 [4096, 128, 1024], P('aux', None, 'vir'), may hold values from -0.024964112 to 0.024964112, as said below
- occupied_energy: float32 [128], P('aux'), may hold values from -3.5 to -2
- virtual_energy: float32 [1024], P('vir'), may hold values from 1.5 to 6
- right_side: float32 [1024, 128], P('vir', 'aux'), may hold values from -500 to 500
Outputs:
- solution: float32 [1024, 128], P('vir', 'aux')
- residual: float32 [1024, 128], P('vir', 'aux')
The draws below stay inside these ranges and needn't reach their ends.
Inputs may be any that keep to these rules, and one draw needn't show every extreme that they name: Entries of the integrals are of order one over the fourth root of 536870912.
All inputs are finite; a program needn't handle non-finite values.
Results may differ from the reference program's by a relative error of at most 0.0003.
Values sent between devices are 32-bit elements; how exact they have to be, the bound alone decides.
No kernel may reach another device: no remote copies, remote signals or barrier semaphores. Data moves between devices by JAX's collectives and lax.ppermute only.
A program may use at most 320 MiB of HBM per device.

```python
import jax
import jax.numpy as jnp
from jax import lax

O = 128
V = 1024
P_SIZE = 4096
ITERS = 3


def draw_integrals(key, part):
    factor = 0.4 ** 0.5 * float(P_SIZE * O * V) ** (-0.25)
    values = jax.random.truncated_normal(key, -3.7, 3.7, (P_SIZE, O, V), jnp.float32)
    return values * factor


def draw_right_side(key, part):
    key_base = jax.random.fold_in(key, 11)
    key_rows = jax.random.fold_in(key, 12)
    key_cols = jax.random.fold_in(key, 13)
    row_scale = 3.0 ** (jnp.arange(V, dtype=jnp.float32) / V) * jnp.exp(jax.random.uniform(key_rows, (V,), jnp.float32, 0.0, 1.2))
    col_scale = 3.0 ** (jnp.arange(O, dtype=jnp.float32) / O) * jnp.exp(jax.random.uniform(key_cols, (O,), jnp.float32, 0.0, 1.2))
    fluctuation = jax.random.truncated_normal(key_base, -5.0, 5.0, (V, O), jnp.float32)
    return fluctuation * row_scale[:, None] * col_scale[None, :]


def level_of(stream_key, shape, pieces, smallest, high):
    def one(axis_at, blocks):
        heights = jax.random.uniform(jax.random.fold_in(jax.random.fold_in(stream_key, 6), axis_at), (blocks,), jnp.float32, smallest / len(pieces), high / len(pieces))
        return jnp.repeat(jnp.exp(heights), shape[axis_at] // blocks).reshape((-1,) + (1,) * (len(shape) - axis_at - 1))

    loudness = one(*pieces[0])
    for cut in pieces[1:]:
        loudness = loudness * one(*cut)
    return loudness


def setup_inputs(seed: int = 0) -> dict:
    splits = jax.random.split(jax.random.key(seed), 5)
    return {
        "integrals": draw_integrals(jax.random.fold_in(splits[4], 71), 0),
        "occupied_energy": jnp.clip(-3.5 + 1.5 * jax.random.uniform(splits[1], (O,), jnp.float32) ** level_of(splits[1], (O,), ((0, 8),), -0.2, 0.2), -3.5, -2.0),
        "virtual_energy": jnp.clip(1.5 + 4.5 * jax.random.uniform(splits[2], (V,), jnp.float32) ** level_of(splits[2], (V,), ((0, 4),), -0.2, 0.2), 1.5, 6.0),
        "right_side": draw_right_side(jax.random.fold_in(splits[4], 71), 0),
    }


HIGHEST = lax.Precision.HIGHEST


def apply_hessian(trial, integrals, energy_gap):
    def block(accumulated, block_ints):
        coulomb = jnp.einsum("pia,ai->p", block_ints, trial, precision=HIGHEST)
        coulomb_term = jnp.einsum("pia,p->ai", block_ints, coulomb, precision=HIGHEST)
        inter = jnp.einsum("pib,bj->pij", block_ints, trial, precision=HIGHEST)
        exchange_term = jnp.einsum("pij,pja->ai", inter, block_ints, precision=HIGHEST)
        return accumulated + 4.0 * coulomb_term - exchange_term, None

    blocks = integrals.reshape(P_SIZE // 128, 128, O, V)
    start = jnp.zeros((V, O), jnp.float32)
    accumulated, _ = lax.scan(block, start, blocks)
    return energy_gap * trial + accumulated


def reference(integrals, occupied_energy, virtual_energy, right_side):
    energy_gap = virtual_energy[:, None] - occupied_energy[None, :]
    solution = jnp.zeros_like(right_side)
    residual = right_side
    direction = right_side
    norm_now = jnp.sum(residual * residual)
    for step in range(ITERS):
        image = apply_hessian(direction, integrals, energy_gap)
        step_len = norm_now / jnp.sum(direction * image)
        solution = solution + step_len * direction
        residual = residual - step_len * image
        norm_next = jnp.sum(residual * residual)
        direction = residual + (norm_next / norm_now) * direction
        norm_now = norm_next
    return solution, residual
```

```python
import functools

import jax
import jax.numpy as jnp
from jax import lax
from jax.experimental import pallas as pl
from jax.experimental.pallas import tpu as pltpu
from jax.sharding import PartitionSpec as P

ITERS = 3
PARTS = (3, 6, 5, 2)
CARRIER = 1
BF16 = jnp.bfloat16
F32 = jnp.float32


def halves(value):
    high = value.astype(BF16)
    return high, (value - high.astype(F32)).astype(BF16)


def load_direction(direction, both):
    occ = direction.shape[0]
    high, low = halves(direction.T)
    both[:, :occ] = high
    both[:, occ:] = low


def coefficients(inter, count):
    occ = inter.shape[1]
    rows = lax.broadcasted_iota(jnp.int32, (occ, occ), 0)
    cols = lax.broadcasted_iota(jnp.int32, (occ, occ), 1)
    diagonal = rows == cols
    highs, lows = [], []
    for p in range(count):
        block = inter[p * occ : (p + 1) * occ]
        trace = jnp.sum(jnp.where(diagonal, block, 0.0))
        high, low = halves(jnp.where(diagonal, 4.0 * trace, 0.0) - block)
        highs.append(high)
        lows.append(low)
    return jnp.concatenate(highs, axis=1), jnp.concatenate(lows, axis=1)


def dot(a, b):
    return jnp.dot(a, b, preferred_element_type=F32)


def first_kernel(first, pieces, direction, *rest):
    if first:
        high_ref, low_ref, total, both = rest
    else:
        before, _, _, high_ref, low_ref, total, both = rest
    groups, count, occ, width = pieces.shape
    rows = count * occ

    @pl.when(pl.program_id(0) == 0)
    def _():
        load_direction(direction[...], both)
        total[...] = jnp.zeros_like(total) if first else before[...]

    inter = jnp.zeros((rows, occ), F32)
    for g in range(groups):
        span = slice(g * width, (g + 1) * width)
        high, low = halves(pieces[g].reshape(rows, width))
        high_ref[:, :, span] = high.reshape(count, occ, width)
        low_ref[:, :, span] = low.reshape(count, occ, width)
        wide = dot(high, both[span, :])
        inter += wide[:, :occ] + wide[:, occ:] + dot(low, both[span, :occ])
    coef_high, coef_low = coefficients(inter, count)
    coef = jnp.concatenate([coef_high, coef_low], axis=0)
    for g in range(groups):
        span = slice(g * width, (g + 1) * width)
        wide = dot(coef, high_ref[:, :, span].reshape(rows, width))
        narrow = dot(coef_high, low_ref[:, :, span].reshape(rows, width))
        total[:, span] += wide[:occ] + wide[occ:] + narrow


def first_part(pieces, direction, before, offset, held, count):
    groups, _, occ, width = pieces.shape
    whole = groups * width
    step = max(s for s in (8, 4, 2, 1) if count % s == 0 and offset % s == 0)
    fixed = pl.BlockSpec((occ, whole), lambda s: (0, 0))
    in_specs = [pl.BlockSpec((groups, step, occ, width), lambda s: (0, s, 0, 0)), fixed]
    args = [pieces, direction]
    aliases = {}
    first = not isinstance(before, tuple)
    if first:
        shape = jax.ShapeDtypeStruct((held, occ, whole), BF16)
    else:
        total, high, low = before
        in_specs += [fixed, pl.BlockSpec(memory_space=pl.ANY), pl.BlockSpec(memory_space=pl.ANY)]
        args += [total, high, low]
        aliases = {3: 0, 4: 1, 2: 2}
        shape = jax.ShapeDtypeStruct(high.shape, BF16)
    start = offset // step
    store = pl.BlockSpec((step, occ, whole), lambda s: (start + s, 0, 0))
    high, low, total = pl.pallas_call(
        functools.partial(first_kernel, first),
        grid=(count // step,),
        in_specs=in_specs,
        out_specs=[store, store, fixed],
        out_shape=[shape, shape, jax.ShapeDtypeStruct((occ, whole), F32)],
        scratch_shapes=[pltpu.VMEM((whole, 2 * occ), BF16)],
        input_output_aliases=aliases,
        compiler_params=pltpu.CompilerParams(vmem_limit_bytes=48 * 1024 * 1024),
    )(*args)
    return total, high, low


def advance(summed, gap, direction, residual, iterate):
    image = gap * direction + summed
    norm = jnp.sum(residual * residual)
    step = norm / jnp.sum(direction * image)
    return iterate + step * direction, residual - step * image, norm


def later_kernel(high_ref, low_ref, summed, gap, direction, residual, iterate,
                 total, new_direction, new_residual, new_iterate, both):
    count, occ, whole = high_ref.shape
    rows = count * occ

    @pl.when(pl.program_id(0) == 0)
    def _():
        point, left, norm = advance(summed[...], gap[...], direction[...], residual[...], iterate[...])
        along = left + (jnp.sum(left * left) / norm) * direction[...]
        new_iterate[...] = point
        new_residual[...] = left
        new_direction[...] = along
        load_direction(along, both)
        total[...] = jnp.zeros_like(total)

    high = high_ref[...].reshape(rows, whole)
    low = low_ref[...].reshape(rows, whole)
    wide = dot(high, both[...])
    inter = wide[:, :occ] + wide[:, occ:] + dot(low, both[:, :occ])
    coef_high, coef_low = coefficients(inter, count)
    coef = jnp.concatenate([coef_high, coef_low], axis=0)
    wide = dot(coef, high)
    total[...] += wide[:occ] + wide[occ:] + dot(coef_high, low)


def later_apply(high, low, *state):
    held, occ, whole = high.shape
    step = max(s for s in (8, 4, 2, 1) if held % s == 0)
    fixed = pl.BlockSpec((occ, whole), lambda s: (0, 0))
    block = pl.BlockSpec((step, occ, whole), lambda s: (s, 0, 0))
    return pl.pallas_call(
        later_kernel,
        grid=(held // step,),
        in_specs=[block, block] + [fixed] * 5,
        out_specs=[fixed] * 4,
        out_shape=[jax.ShapeDtypeStruct((occ, whole), F32)] * 4,
        scratch_shapes=[pltpu.VMEM((whole, 2 * occ), BF16)],
        compiler_params=pltpu.CompilerParams(vmem_limit_bytes=48 * 1024 * 1024),
    )(high, low, *state)


def on_device(groups, integrals, occupied_energy, virtual_energy, right_side):
    aux_rows, occ, width = integrals.shape
    whole = groups * width
    unit = aux_rows // groups // sum(PARTS)

    mine = occupied_energy.shape[0]
    sent = jnp.concatenate(
        [right_side.T, jnp.broadcast_to(occupied_energy[:, None], (mine, 128))], axis=1
    )
    columns = lax.all_gather(sent, "aux", axis=0, tiled=True)
    carried = jnp.stack(
        [columns[:, :width], virtual_energy[None, :] - columns[:, width : width + 1]]
    )

    received = []
    low_row = 0
    for k, share in enumerate(PARTS):
        count = share * unit
        part = integrals[low_row : low_row + groups * count].reshape(groups, count, occ, width)
        low_row += groups * count
        if k == CARRIER:
            extra = jnp.broadcast_to(carried[None], (groups,) + carried.shape)
            part = jnp.concatenate([part, extra], axis=1)
        if k >= 2:
            part, _ = lax.optimization_barrier((part, received[k - 2]))
        received.append(lax.all_to_all(part, "vir", split_axis=0, concat_axis=0, tiled=True))

    at = PARTS[CARRIER] * unit
    start, gap = (
        jnp.moveaxis(received[CARRIER][:, at + n], 0, 1).reshape(occ, whole) for n in range(2)
    )
    held = None
    offset = 0
    for k, share in enumerate(PARTS):
        count = share * unit
        held = first_part(received[k], start, held, offset, aux_rows // groups, count)
        offset += count
    total, high, low = held

    direction = residual = start
    iterate = jnp.zeros_like(start)
    for _ in range(ITERS - 1):
        summed = lax.psum(total, ("aux", "vir"))
        total, direction, residual, iterate = later_apply(
            high, low, summed, gap, direction, residual, iterate
        )
    summed = lax.psum(total, ("aux", "vir"))
    iterate, residual, _ = advance(summed, gap, direction, residual, iterate)

    def own(array):
        block = lax.dynamic_slice(
            array, (lax.axis_index("aux") * mine, lax.axis_index("vir") * width), (mine, width)
        )
        return block.T

    return own(iterate), own(residual)


def solution(mesh):
    in_specs = (P("aux", None, "vir"), P("aux"), P("vir"), P("vir", "aux"))
    out_specs = (P("vir", "aux"), P("vir", "aux"))
    return jax.shard_map(
        functools.partial(on_device, mesh.shape["vir"]),
        mesh=mesh,
        in_specs=in_specs,
        out_specs=out_specs,
        check_vma=False,
    )
```

```python
import functools

import jax
import jax.numpy as jnp
from jax import lax
from jax.experimental import pallas as pl
from jax.experimental.pallas import tpu as pltpu
from jax.sharding import PartitionSpec as P

ITERS = 3
PARTS = (4, 4, 4, 2, 2)
CARRIER = 1
BF16 = jnp.bfloat16
F32 = jnp.float32


def halves(value):
    high = value.astype(BF16)
    return high, (value - high.astype(F32)).astype(BF16)


def load_direction(direction, both):
    occ = direction.shape[0]
    high, low = halves(direction.T)
    both[:, :occ] = high
    both[:, occ:] = low


def coefficients(inter, count):
    occ = inter.shape[1]
    rows = lax.broadcasted_iota(jnp.int32, (occ, occ), 0)
    cols = lax.broadcasted_iota(jnp.int32, (occ, occ), 1)
    diagonal = rows == cols
    highs, lows = [], []
    for p in range(count):
        block = inter[p * occ : (p + 1) * occ]
        trace = jnp.sum(jnp.where(diagonal, block, 0.0))
        high, low = halves(jnp.where(diagonal, 4.0 * trace, 0.0) - block)
        highs.append(high)
        lows.append(low)
    return jnp.concatenate(highs, axis=1), jnp.concatenate(lows, axis=1)


def dot(a, b):
    return jnp.dot(a, b, preferred_element_type=F32)


def first_kernel(first, groups, *refs):
    pieces, direction, rest = refs[:groups], refs[groups], refs[groups + 1 :]
    if first:
        high_ref, low_ref, total, both = rest
    else:
        before, _, _, high_ref, low_ref, total, both = rest
    count, occ, width = pieces[0].shape
    rows = count * occ
    me = lax.axis_index("vir")

    def columns(shift):
        source = lax.rem(me - shift + groups, groups)
        return pl.ds(pl.multiple_of(source * width, width), width)

    @pl.when(pl.program_id(0) == 0)
    def _():
        load_direction(direction[...], both)
        total[...] = jnp.zeros_like(total) if first else before[...]

    inter = jnp.zeros((rows, occ), F32)
    for shift in range(groups):
        span = columns(shift)
        high, low = halves(pieces[shift][...].reshape(rows, width))
        high_ref[:, :, span] = high.reshape(count, occ, width)
        low_ref[:, :, span] = low.reshape(count, occ, width)
        wide = dot(high, both[span, :])
        inter += wide[:, :occ] + wide[:, occ:] + dot(low, both[span, :occ])
    coef_high, coef_low = coefficients(inter, count)
    coef = jnp.concatenate([coef_high, coef_low], axis=0)
    for shift in range(groups):
        span = columns(shift)
        wide = dot(coef, high_ref[:, :, span].reshape(rows, width))
        narrow = dot(coef_high, low_ref[:, :, span].reshape(rows, width))
        total[:, span] += wide[:occ] + wide[occ:] + narrow


def first_part(pieces, direction, before, offset, held):
    groups = len(pieces)
    count, occ, width = pieces[0].shape
    whole = groups * width
    step = max(s for s in (8, 4, 2, 1) if count % s == 0 and offset % s == 0)
    fixed = pl.BlockSpec((occ, whole), lambda s: (0, 0))
    in_specs = [pl.BlockSpec((step, occ, width), lambda s: (s, 0, 0))] * groups + [fixed]
    args = [*pieces, direction]
    aliases = {}
    first = before is None
    if first:
        shape = jax.ShapeDtypeStruct((held, occ, whole), BF16)
    else:
        total, high, low = before
        in_specs += [fixed, pl.BlockSpec(memory_space=pl.ANY), pl.BlockSpec(memory_space=pl.ANY)]
        args += [total, high, low]
        aliases = {groups + 2: 0, groups + 3: 1, groups + 1: 2}
        shape = jax.ShapeDtypeStruct(high.shape, BF16)
    start = offset // step
    store = pl.BlockSpec((step, occ, whole), lambda s: (start + s, 0, 0))
    high, low, total = pl.pallas_call(
        functools.partial(first_kernel, first, groups),
        grid=(count // step,),
        in_specs=in_specs,
        out_specs=[store, store, fixed],
        out_shape=[shape, shape, jax.ShapeDtypeStruct((occ, whole), F32)],
        scratch_shapes=[pltpu.VMEM((whole, 2 * occ), BF16)],
        input_output_aliases=aliases,
        compiler_params=pltpu.CompilerParams(vmem_limit_bytes=48 * 1024 * 1024),
    )(*args)
    return total, high, low


def advance(summed, gap, direction, residual, iterate):
    image = gap * direction + summed
    norm = jnp.sum(residual * residual)
    step = norm / jnp.sum(direction * image)
    return iterate + step * direction, residual - step * image, norm


def later_kernel(high_ref, low_ref, summed, gap, direction, residual, iterate,
                 total, new_direction, new_residual, new_iterate, both):
    count, occ, whole = high_ref.shape
    rows = count * occ

    @pl.when(pl.program_id(0) == 0)
    def _():
        point, left, norm = advance(summed[...], gap[...], direction[...], residual[...], iterate[...])
        along = left + (jnp.sum(left * left) / norm) * direction[...]
        new_iterate[...] = point
        new_residual[...] = left
        new_direction[...] = along
        load_direction(along, both)
        total[...] = jnp.zeros_like(total)

    high = high_ref[...].reshape(rows, whole)
    low = low_ref[...].reshape(rows, whole)
    wide = dot(high, both[...])
    inter = wide[:, :occ] + wide[:, occ:] + dot(low, both[:, :occ])
    coef_high, coef_low = coefficients(inter, count)
    coef = jnp.concatenate([coef_high, coef_low], axis=0)
    wide = dot(coef, high)
    total[...] += wide[:occ] + wide[occ:] + dot(coef_high, low)


def later_apply(high, low, *state):
    held, occ, whole = high.shape
    step = max(s for s in (8, 4, 2, 1) if held % s == 0)
    fixed = pl.BlockSpec((occ, whole), lambda s: (0, 0))
    block = pl.BlockSpec((step, occ, whole), lambda s: (s, 0, 0))
    return pl.pallas_call(
        later_kernel,
        grid=(held // step,),
        in_specs=[block, block] + [fixed] * 5,
        out_specs=[fixed] * 4,
        out_shape=[jax.ShapeDtypeStruct((occ, whole), F32)] * 4,
        scratch_shapes=[pltpu.VMEM((whole, 2 * occ), BF16)],
        compiler_params=pltpu.CompilerParams(vmem_limit_bytes=48 * 1024 * 1024),
    )(high, low, *state)


def add_over(pieces, axes):
    return jnp.sum(lax.all_to_all(pieces, axes, split_axis=0, concat_axis=0, tiled=True), axis=0)


def all_at_once(total, mine, width):
    occ, whole = total.shape
    blocks = jnp.swapaxes(total.reshape(occ // mine, mine, whole // width, width), 1, 2)
    block = add_over(blocks.reshape(-1, mine, width), ("aux", "vir"))
    blocks = lax.all_gather(block, ("aux", "vir"), axis=0)
    blocks = blocks.reshape(occ // mine, whole // width, mine, width)
    return jnp.swapaxes(blocks, 1, 2).reshape(occ, whole)


def axis_by_axis(total, mine, width):
    occ, whole = total.shape
    rows = add_over(total.reshape(occ // mine, mine, whole), "aux")
    block = add_over(jnp.swapaxes(rows.reshape(mine, whole // width, width), 0, 1), "vir")
    rows = jnp.swapaxes(lax.all_gather(block, "vir", axis=0), 0, 1).reshape(mine, whole)
    return lax.all_gather(rows, "aux", axis=0, tiled=True)


def on_device(groups, integrals, occupied_energy, virtual_energy, right_side):
    aux_rows, occ, width = integrals.shape
    whole = groups * width
    unit = aux_rows // groups // sum(PARTS)
    mine = occupied_energy.shape[0]
    me = lax.axis_index("vir")

    sent = jnp.concatenate(
        [right_side.T, jnp.broadcast_to(occupied_energy[:, None], (mine, 128))], axis=1
    )
    columns = lax.all_gather(sent, "aux", axis=0, tiled=True)
    carried = jnp.stack(
        [columns[:, :width], virtual_energy[None, :] - columns[:, width : width + 1]]
    )

    def shifted(array, shift):
        return lax.ppermute(array, "vir", [(z, (z + shift) % groups) for z in range(groups)])

    received = []
    low_row = 0
    for k, share in enumerate(PARTS):
        count = share * unit
        blocks = [
            lax.dynamic_slice_in_dim(
                integrals, low_row + lax.rem(me + shift, groups) * count, count, axis=0
            )
            for shift in range(groups)
        ]
        low_row += groups * count
        if k >= 2:
            blocks, _ = lax.optimization_barrier((blocks, received[k - 2]))
        received.append(blocks[:1] + [shifted(blocks[n], n) for n in range(1, groups)])
        if k == CARRIER:
            spread = jnp.zeros((groups,) + carried.shape, F32)
            for shift in range(groups):
                piece = carried if shift == 0 else shifted(carried, shift)
                source = lax.rem(me - shift + groups, groups)
                spread = lax.dynamic_update_index_in_dim(spread, piece, source, 0)
    start, gap = (jnp.moveaxis(spread[:, n], 0, 1).reshape(occ, whole) for n in range(2))

    held = None
    offset = 0
    for pieces in received:
        held = first_part(pieces, start, held, offset, aux_rows // groups)
        offset += pieces[0].shape[0]
    total, high, low = held

    direction = residual = start
    iterate = jnp.zeros_like(start)
    for step in range(ITERS - 1):
        add_up = all_at_once if step == 0 else axis_by_axis
        summed = add_up(total, mine, width)
        total, direction, residual, iterate = later_apply(
            high, low, summed, gap, direction, residual, iterate
        )

    def own(array):
        return lax.dynamic_slice(array, (lax.axis_index("aux") * mine, me * width), (mine, width))

    product = jnp.full((occ // mine, groups, 1, width), jnp.sum(direction * total), F32)
    blocks = jnp.swapaxes(total.reshape(occ // mine, mine, groups, width), 1, 2)
    blocks = jnp.concatenate([blocks, product], axis=2).reshape(-1, mine + 1, width)
    block = add_over(blocks, ("aux", "vir"))
    product = block[mine, 0] + jnp.sum(gap * direction * direction)
    size = jnp.sum(residual * residual) / product
    image = own(gap) * own(direction) + block[:mine]
    iterate = own(iterate) + size * own(direction)
    residual = own(residual) - size * image
    return iterate.T, residual.T


def solution(mesh):
    in_specs = (P("aux", None, "vir"), P("aux"), P("vir"), P("vir", "aux"))
    out_specs = (P("vir", "aux"), P("vir", "aux"))
    return jax.shard_map(
        functools.partial(on_device, mesh.shape["vir"]),
        mesh=mesh,
        in_specs=in_specs,
        out_specs=out_specs,
        check_vma=False,
    )
```

```python
import functools

import jax
import jax.numpy as jnp
from jax import lax
from jax.experimental import pallas as pl
from jax.experimental.pallas import tpu as pltpu
from jax.sharding import PartitionSpec as P

ITERS = 3
PARTS = (1, 4, 4, 4, 2, 1)
CARRIER = 1
BF16 = jnp.bfloat16
F32 = jnp.float32


def halves(value):
    high = value.astype(BF16)
    return high, (value - high.astype(F32)).astype(BF16)


def load_direction(direction, both):
    occ = direction.shape[0]
    high, low = halves(direction.T)
    both[:, :occ] = high
    both[:, occ:] = low


def coefficients(inter, count):
    occ = inter.shape[1]
    rows = lax.broadcasted_iota(jnp.int32, (occ, occ), 0)
    cols = lax.broadcasted_iota(jnp.int32, (occ, occ), 1)
    diagonal = rows == cols
    highs, lows = [], []
    for p in range(count):
        block = inter[p * occ : (p + 1) * occ]
        trace = jnp.sum(jnp.where(diagonal, block, 0.0))
        high, low = halves(jnp.where(diagonal, 4.0 * trace, 0.0) - block)
        highs.append(high)
        lows.append(low)
    return jnp.concatenate(highs, axis=1), jnp.concatenate(lows, axis=1)


def dot(a, b):
    return jnp.dot(a, b, preferred_element_type=F32)


def first_kernel(first, groups, *refs):
    pieces, direction, rest = refs[:groups], refs[groups], refs[groups + 1 :]
    if first:
        high_ref, low_ref, total, both = rest
    else:
        before, _, _, high_ref, low_ref, total, both = rest
    count, occ, width = pieces[0].shape
    rows = count * occ
    me = lax.axis_index("vir")

    def columns(shift):
        source = lax.rem(me - shift + groups, groups)
        return pl.ds(pl.multiple_of(source * width, width), width)

    @pl.when(pl.program_id(0) == 0)
    def _():
        load_direction(direction[...], both)
        total[...] = jnp.zeros_like(total) if first else before[...]

    inter = jnp.zeros((rows, occ), F32)
    for shift in range(groups):
        span = columns(shift)
        high, low = halves(pieces[shift][...].reshape(rows, width))
        high_ref[:, :, span] = high.reshape(count, occ, width)
        low_ref[:, :, span] = low.reshape(count, occ, width)
        wide = dot(high, both[span, :])
        inter += wide[:, :occ] + wide[:, occ:] + dot(low, both[span, :occ])
    coef_high, coef_low = coefficients(inter, count)
    coef = jnp.concatenate([coef_high, coef_low], axis=0)
    for shift in range(groups):
        span = columns(shift)
        wide = dot(coef, high_ref[:, :, span].reshape(rows, width))
        narrow = dot(coef_high, low_ref[:, :, span].reshape(rows, width))
        total[:, span] += wide[:occ] + wide[occ:] + narrow


def first_part(pieces, direction, before, offset, held):
    groups = len(pieces)
    count, occ, width = pieces[0].shape
    whole = groups * width
    step = max(s for s in (8, 4, 2, 1) if count % s == 0 and offset % s == 0)
    fixed = pl.BlockSpec((occ, whole), lambda s: (0, 0))
    in_specs = [pl.BlockSpec((step, occ, width), lambda s: (s, 0, 0))] * groups + [fixed]
    args = [*pieces, direction]
    aliases = {}
    first = before is None
    if first:
        shape = jax.ShapeDtypeStruct((held, occ, whole), BF16)
    else:
        total, high, low = before
        in_specs += [fixed, pl.BlockSpec(memory_space=pl.ANY), pl.BlockSpec(memory_space=pl.ANY)]
        args += [total, high, low]
        aliases = {groups + 2: 0, groups + 3: 1, groups + 1: 2}
        shape = jax.ShapeDtypeStruct(high.shape, BF16)
    start = offset // step
    store = pl.BlockSpec((step, occ, whole), lambda s: (start + s, 0, 0))
    high, low, total = pl.pallas_call(
        functools.partial(first_kernel, first, groups),
        grid=(count // step,),
        in_specs=in_specs,
        out_specs=[store, store, fixed],
        out_shape=[shape, shape, jax.ShapeDtypeStruct((occ, whole), F32)],
        scratch_shapes=[pltpu.VMEM((whole, 2 * occ), BF16)],
        input_output_aliases=aliases,
        compiler_params=pltpu.CompilerParams(vmem_limit_bytes=48 * 1024 * 1024),
    )(*args)
    return total, high, low


def advance(summed, gap, direction, residual, iterate):
    image = gap * direction + summed
    norm = jnp.sum(residual * residual)
    step = norm / jnp.sum(direction * image)
    return iterate + step * direction, residual - step * image, norm


def later_kernel(high_ref, low_ref, summed, gap, direction, residual, iterate,
                 total, new_direction, new_residual, new_iterate, both):
    count, occ, whole = high_ref.shape

    @pl.when(pl.program_id(0) == 0)
    def _():
        point, left, norm = advance(summed[...], gap[...], direction[...], residual[...], iterate[...])
        along = left + (jnp.sum(left * left) / norm) * direction[...]
        new_iterate[...] = point
        new_residual[...] = left
        new_direction[...] = along
        load_direction(along, both)
        total[...] = jnp.zeros_like(total)

    spans = [slice(n * (count // 2), (n + 1) * (count // 2)) for n in range(2)] if count > 1 else [slice(0, 1)]
    inters = []
    for span in spans:
        wide = dot(high_ref[span].reshape(-1, whole), both[...])
        narrow = dot(low_ref[span].reshape(-1, whole), both[:, :occ])
        inters.append(wide[:, :occ] + wide[:, occ:] + narrow)
    for span, inter in zip(spans, inters):
        coef_high, coef_low = coefficients(inter, span.stop - span.start)
        coef = jnp.concatenate([coef_high, coef_low], axis=0)
        wide = dot(coef, high_ref[span].reshape(-1, whole))
        narrow = dot(coef_high, low_ref[span].reshape(-1, whole))
        total[...] += wide[:occ] + wide[occ:] + narrow


def later_apply(high, low, *state):
    held, occ, whole = high.shape
    step = max(s for s in (16, 8, 4, 2, 1) if held % s == 0)
    fixed = pl.BlockSpec((occ, whole), lambda s: (0, 0))
    block = pl.BlockSpec((step, occ, whole), lambda s: (s, 0, 0))
    return pl.pallas_call(
        later_kernel,
        grid=(held // step,),
        in_specs=[block, block] + [fixed] * 5,
        out_specs=[fixed] * 4,
        out_shape=[jax.ShapeDtypeStruct((occ, whole), F32)] * 4,
        scratch_shapes=[pltpu.VMEM((whole, 2 * occ), BF16)],
        compiler_params=pltpu.CompilerParams(vmem_limit_bytes=48 * 1024 * 1024),
    )(high, low, *state)


def add_over(pieces, axes):
    return jnp.sum(lax.all_to_all(pieces, axes, split_axis=0, concat_axis=0, tiled=True), axis=0)


def add_up(total, mine, groups):
    occ, whole = total.shape
    rows = add_over(total.reshape(occ // mine, mine, whole), "aux")
    rows = add_over(jnp.broadcast_to(rows[None], (groups, mine, whole)), "vir")
    return lax.all_gather(rows, "aux", axis=0, tiled=True)


def on_device(groups, integrals, occupied_energy, virtual_energy, right_side):
    aux_rows, occ, width = integrals.shape
    whole = groups * width
    unit = aux_rows // groups // sum(PARTS)
    mine = occupied_energy.shape[0]
    me = lax.axis_index("vir")

    sent = jnp.concatenate(
        [right_side.T, jnp.broadcast_to(occupied_energy[:, None], (mine, 128))], axis=1
    )
    columns = lax.all_gather(sent, "aux", axis=0, tiled=True)
    carried = jnp.stack(
        [columns[:, :width], virtual_energy[None, :] - columns[:, width : width + 1]]
    )

    def shifted(array, shift):
        return lax.ppermute(array, "vir", [(z, (z + shift) % groups) for z in range(groups)])

    received = []
    low_row = 0
    for k, share in enumerate(PARTS):
        count = share * unit
        blocks = [
            lax.dynamic_slice_in_dim(
                integrals, low_row + lax.rem(me + shift, groups) * count, count, axis=0
            )
            for shift in range(groups)
        ]
        low_row += groups * count
        if k == 0:
            blocks, integrals = lax.optimization_barrier((blocks, integrals))
        elif k >= 2:
            blocks, _ = lax.optimization_barrier((blocks, received[k - 2]))
        received.append(blocks[:1] + [shifted(blocks[n], n) for n in range(1, groups)])
        if k == CARRIER:
            spread = jnp.zeros((groups,) + carried.shape, F32)
            for shift in range(groups):
                piece = carried if shift == 0 else shifted(carried, shift)
                source = lax.rem(me - shift + groups, groups)
                spread = lax.dynamic_update_index_in_dim(spread, piece, source, 0)
    start, gap = (jnp.moveaxis(spread[:, n], 0, 1).reshape(occ, whole) for n in range(2))

    held = None
    offset = 0
    for pieces in received:
        held = first_part(pieces, start, held, offset, aux_rows // groups)
        offset += pieces[0].shape[0]
    total, high, low = held

    direction = residual = start
    iterate = jnp.zeros_like(start)
    for _ in range(ITERS - 1):
        summed = add_up(total, mine, groups)
        total, direction, residual, iterate = later_apply(
            high, low, summed, gap, direction, residual, iterate
        )

    def own(array):
        return lax.dynamic_slice(array, (lax.axis_index("aux") * mine, me * width), (mine, width))

    product = jnp.full((occ // mine, groups, 1, width), jnp.sum(direction * total), F32)
    blocks = jnp.swapaxes(total.reshape(occ // mine, mine, groups, width), 1, 2)
    blocks = jnp.concatenate([blocks, product], axis=2).reshape(-1, mine + 1, width)
    block = add_over(blocks, ("aux", "vir"))
    product = block[mine, 0] + jnp.sum(gap * direction * direction)
    size = jnp.sum(residual * residual) / product
    image = own(gap) * own(direction) + block[:mine]
    iterate = own(iterate) + size * own(direction)
    residual = own(residual) - size * image
    return iterate.T, residual.T


def solution(mesh):
    in_specs = (P("aux", None, "vir"), P("aux"), P("vir"), P("vir", "aux"))
    out_specs = (P("vir", "aux"), P("vir", "aux"))
    return jax.shard_map(
        functools.partial(on_device, mesh.shape["vir"]),
        mesh=mesh,
        in_specs=in_specs,
        out_specs=out_specs,
        check_vma=False,
    )
```

```python
import functools

import jax
import jax.numpy as jnp
from jax import lax
from jax.experimental import pallas as pl
from jax.experimental.pallas import tpu as pltpu
from jax.sharding import PartitionSpec as P

ITERS = 3
PARTS = (1, 2, 4, 4, 4, 1)
CARRIER = 2
BF16 = jnp.bfloat16
F32 = jnp.float32


def halves(value):
    high = value.astype(BF16)
    return high, (value - high.astype(F32)).astype(BF16)


def load_direction(direction, both):
    occ = direction.shape[0]
    high, low = halves(direction.T)
    both[:, :occ] = high
    both[:, occ:] = low


def coefficients(inter, count):
    occ = inter.shape[1]
    rows = lax.broadcasted_iota(jnp.int32, (occ, occ), 0)
    cols = lax.broadcasted_iota(jnp.int32, (occ, occ), 1)
    diagonal = rows == cols
    highs, lows = [], []
    for p in range(count):
        block = inter[p * occ : (p + 1) * occ]
        trace = jnp.sum(jnp.where(diagonal, block, 0.0))
        high, low = halves(jnp.where(diagonal, 4.0 * trace, 0.0) - block)
        highs.append(high)
        lows.append(low)
    return jnp.concatenate(highs, axis=1), jnp.concatenate(lows, axis=1)


def dot(a, b):
    return jnp.dot(a, b, preferred_element_type=F32)


def first_kernel(first, groups, *refs):
    pieces, direction, rest = refs[:groups], refs[groups], refs[groups + 1 :]
    if first:
        high_ref, low_ref, total, both = rest
    else:
        before, _, _, high_ref, low_ref, total, both = rest
    count, occ, width = pieces[0].shape
    rows = count * occ
    me = lax.axis_index("vir")

    def columns(shift):
        source = lax.rem(me - shift + groups, groups)
        return pl.ds(pl.multiple_of(source * width, width), width)

    @pl.when(pl.program_id(0) == 0)
    def _():
        load_direction(direction[...], both)
        total[...] = jnp.zeros_like(total) if first else before[...]

    inter = jnp.zeros((rows, occ), F32)
    for shift in range(groups):
        span = columns(shift)
        high, low = halves(pieces[shift][...].reshape(rows, width))
        high_ref[:, :, span] = high.reshape(count, occ, width)
        low_ref[:, :, span] = low.reshape(count, occ, width)
        wide = dot(high, both[span, :])
        inter += wide[:, :occ] + wide[:, occ:] + dot(low, both[span, :occ])
    coef_high, coef_low = coefficients(inter, count)
    coef = jnp.concatenate([coef_high, coef_low], axis=0)
    for shift in range(groups):
        span = columns(shift)
        wide = dot(coef, high_ref[:, :, span].reshape(rows, width))
        narrow = dot(coef_high, low_ref[:, :, span].reshape(rows, width))
        total[:, span] += wide[:occ] + wide[occ:] + narrow


def first_part(pieces, direction, before, offset, held):
    groups = len(pieces)
    count, occ, width = pieces[0].shape
    whole = groups * width
    step = max(s for s in (8, 4, 2, 1) if count % s == 0 and offset % s == 0)
    fixed = pl.BlockSpec((occ, whole), lambda s: (0, 0))
    in_specs = [pl.BlockSpec((step, occ, width), lambda s: (s, 0, 0))] * groups + [fixed]
    args = [*pieces, direction]
    aliases = {}
    first = before is None
    if first:
        shape = jax.ShapeDtypeStruct((held, occ, whole), BF16)
    else:
        total, high, low = before
        in_specs += [fixed, pl.BlockSpec(memory_space=pl.ANY), pl.BlockSpec(memory_space=pl.ANY)]
        args += [total, high, low]
        aliases = {groups + 2: 0, groups + 3: 1, groups + 1: 2}
        shape = jax.ShapeDtypeStruct(high.shape, BF16)
    start = offset // step
    store = pl.BlockSpec((step, occ, whole), lambda s: (start + s, 0, 0))
    high, low, total = pl.pallas_call(
        functools.partial(first_kernel, first, groups),
        grid=(count // step,),
        in_specs=in_specs,
        out_specs=[store, store, fixed],
        out_shape=[shape, shape, jax.ShapeDtypeStruct((occ, whole), F32)],
        scratch_shapes=[pltpu.VMEM((whole, 2 * occ), BF16)],
        input_output_aliases=aliases,
        compiler_params=pltpu.CompilerParams(vmem_limit_bytes=48 * 1024 * 1024),
    )(*args)
    return total, high, low


def advance(summed, gap, direction, residual, iterate):
    image = gap * direction + summed
    norm = jnp.sum(residual * residual)
    step = norm / jnp.sum(direction * image)
    return iterate + step * direction, residual - step * image, norm


def later_kernel(high_ref, low_ref, summed, gap, direction, residual, iterate,
                 total, new_direction, new_residual, new_iterate, both):
    count, occ, whole = high_ref.shape

    @pl.when(pl.program_id(0) == 0)
    def _():
        point, left, norm = advance(summed[...], gap[...], direction[...], residual[...], iterate[...])
        along = left + (jnp.sum(left * left) / norm) * direction[...]
        new_iterate[...] = point
        new_residual[...] = left
        new_direction[...] = along
        load_direction(along, both)
        total[...] = jnp.zeros_like(total)

    spans = [slice(n * (count // 2), (n + 1) * (count // 2)) for n in range(2)] if count > 1 else [slice(0, 1)]
    inters = []
    for span in spans:
        wide = dot(high_ref[span].reshape(-1, whole), both[...])
        narrow = dot(low_ref[span].reshape(-1, whole), both[:, :occ])
        inters.append(wide[:, :occ] + wide[:, occ:] + narrow)
    for span, inter in zip(spans, inters):
        coef_high, coef_low = coefficients(inter, span.stop - span.start)
        coef = jnp.concatenate([coef_high, coef_low], axis=0)
        wide = dot(coef, high_ref[span].reshape(-1, whole))
        narrow = dot(coef_high, low_ref[span].reshape(-1, whole))
        total[...] += wide[:occ] + wide[occ:] + narrow


def later_apply(high, low, *state):
    held, occ, whole = high.shape
    step = max(s for s in (16, 8, 4, 2, 1) if held % s == 0)
    fixed = pl.BlockSpec((occ, whole), lambda s: (0, 0))
    block = pl.BlockSpec((step, occ, whole), lambda s: (s, 0, 0))
    return pl.pallas_call(
        later_kernel,
        grid=(held // step,),
        in_specs=[block, block] + [fixed] * 5,
        out_specs=[fixed] * 4,
        out_shape=[jax.ShapeDtypeStruct((occ, whole), F32)] * 4,
        scratch_shapes=[pltpu.VMEM((whole, 2 * occ), BF16)],
        compiler_params=pltpu.CompilerParams(vmem_limit_bytes=48 * 1024 * 1024),
    )(high, low, *state)


def add_over(pieces, axes):
    return jnp.sum(lax.all_to_all(pieces, axes, split_axis=0, concat_axis=0, tiled=True), axis=0)


def add_up(total, mine, groups):
    occ, whole = total.shape
    rows = add_over(total.reshape(occ // mine, mine, whole), "aux")
    rows = add_over(jnp.broadcast_to(rows[None], (groups, mine, whole)), "vir")
    return lax.all_gather(rows, "aux", axis=0, tiled=True)


def on_device(groups, integrals, occupied_energy, virtual_energy, right_side):
    aux_rows, occ, width = integrals.shape
    whole = groups * width
    unit = aux_rows // groups // sum(PARTS)
    mine = occupied_energy.shape[0]
    me = lax.axis_index("vir")

    def start_and_gaps(earlier):
        first, occupied, _ = lax.optimization_barrier((right_side, occupied_energy, earlier))
        rows = jnp.concatenate(
            [first.T, jnp.broadcast_to(occupied[:, None], (mine, 128))], axis=1
        )
        rows = lax.all_gather(rows, "aux", axis=0, tiled=True)
        return jnp.stack([rows[:, :width], virtual_energy[None, :] - rows[:, width : width + 1]])

    def shifted(array, shift):
        return lax.ppermute(array, "vir", [(z, (z + shift) % groups) for z in range(groups)])

    def by_source(pieces):
        turned = pieces[:0:-1] + pieces[:1]
        twice = jnp.concatenate(turned + turned[:-1], axis=1)
        return lax.dynamic_slice(twice, (0, (groups - 1 - me) * width), (occ, whole))

    received = []
    held = start = None
    low_row = offset = 0

    def apply_part(k):
        nonlocal held, offset
        held = first_part(received[k], start, held, offset, aux_rows // groups)
        offset += PARTS[k] * unit

    for k, share in enumerate(PARTS):
        count = share * unit
        if k == CARRIER + 2:
            for n in range(k - 1):
                apply_part(n)
        elif k > CARRIER + 2:
            apply_part(k - 2)
        if held is not None:
            total, high, low = held
            integrals, total, start, gap = lax.optimization_barrier((integrals, total, start, gap))
            held = total, high, low
        elif k >= 2:
            integrals, _ = lax.optimization_barrier((integrals, received[k - 2]))
        blocks = [
            lax.dynamic_slice_in_dim(
                integrals, low_row + lax.rem(me + shift, groups) * count, count, axis=0
            )
            for shift in range(groups)
        ]
        low_row += groups * count
        if k == 0:
            blocks, integrals = lax.optimization_barrier((blocks, integrals))
        sent = blocks[1:]
        if k == CARRIER:
            carried = start_and_gaps(received[0][1])
            sent = [jnp.concatenate([block, carried], axis=0) for block in sent]
        arrived = [shifted(block, n) for n, block in enumerate(sent, 1)]
        received.append(blocks[:1] + arrived)
        if k == CARRIER:
            own_and_others = [carried] + [piece[count:] for piece in arrived]
            start, gap = (by_source([piece[n] for piece in own_and_others]) for n in range(2))
    for k in range(len(PARTS) - 2, len(PARTS)):
        apply_part(k)
    total, high, low = held

    direction = residual = start
    iterate = jnp.zeros_like(start)
    for _ in range(ITERS - 1):
        summed = add_up(total, mine, groups)
        total, direction, residual, iterate = later_apply(
            high, low, summed, gap, direction, residual, iterate
        )

    def own(array):
        return lax.dynamic_slice(array, (lax.axis_index("aux") * mine, me * width), (mine, width))

    product = jnp.full((occ // mine, groups, 1, width), jnp.sum(direction * total), F32)
    blocks = jnp.swapaxes(total.reshape(occ // mine, mine, groups, width), 1, 2)
    blocks = jnp.concatenate([blocks, product], axis=2).reshape(-1, mine + 1, width)
    block = add_over(blocks, ("aux", "vir"))
    product = block[mine, 0] + jnp.sum(gap * direction * direction)
    size = jnp.sum(residual * residual) / product
    image = own(gap) * own(direction) + block[:mine]
    iterate = own(iterate) + size * own(direction)
    residual = own(residual) - size * image
    return iterate.T, residual.T


def solution(mesh):
    in_specs = (P("aux", None, "vir"), P("aux"), P("vir"), P("vir", "aux"))
    out_specs = (P("vir", "aux"), P("vir", "aux"))
    return jax.shard_map(
        functools.partial(on_device, mesh.shape["vir"]),
        mesh=mesh,
        in_specs=in_specs,
        out_specs=out_specs,
        check_vma=False,
    )
```

```python
import functools

import jax
import jax.numpy as jnp
from jax import lax
from jax.experimental import pallas as pl
from jax.experimental.pallas import tpu as pltpu
from jax.sharding import PartitionSpec as P

ITERS = 3
PARTS = (1, 2, 2, 3, 3, 2, 2, 1)
CARRIER = 2
DEPTH = 3
BF16 = jnp.bfloat16
F32 = jnp.float32


def halves(value):
    high = value.astype(BF16)
    return high, (value - high.astype(F32)).astype(BF16)


def load_direction(direction, both):
    occ = direction.shape[0]
    high, low = halves(direction.T)
    both[:, :occ] = high
    both[:, occ:] = low


def coefficients(inter, count):
    occ = inter.shape[1]
    rows = lax.broadcasted_iota(jnp.int32, (occ, occ), 0)
    cols = lax.broadcasted_iota(jnp.int32, (occ, occ), 1)
    diagonal = rows == cols
    highs, lows = [], []
    for p in range(count):
        block = inter[p * occ : (p + 1) * occ]
        trace = jnp.sum(jnp.where(diagonal, block, 0.0))
        high, low = halves(jnp.where(diagonal, 4.0 * trace, 0.0) - block)
        highs.append(high)
        lows.append(low)
    return jnp.concatenate(highs, axis=1), jnp.concatenate(lows, axis=1)


def dot(a, b):
    return jnp.dot(a, b, preferred_element_type=F32)


def first_kernel(first, groups, *refs):
    pieces, direction, rest = refs[:groups], refs[groups], refs[groups + 1 :]
    if first:
        high_ref, low_ref, total, both = rest
    else:
        before, _, _, high_ref, low_ref, total, both = rest
    count, occ, width = pieces[0].shape
    rows = count * occ
    me = lax.axis_index("vir")

    def columns(shift):
        source = lax.rem(me - shift + groups, groups)
        return pl.ds(pl.multiple_of(source * width, width), width)

    @pl.when(pl.program_id(0) == 0)
    def _():
        load_direction(direction[...], both)
        total[...] = jnp.zeros_like(total) if first else before[...]

    inter = jnp.zeros((rows, occ), F32)
    for shift in range(groups):
        span = columns(shift)
        high, low = halves(pieces[shift][...].reshape(rows, width))
        high_ref[:, :, span] = high.reshape(count, occ, width)
        low_ref[:, :, span] = low.reshape(count, occ, width)
        wide = dot(high, both[span, :])
        inter += wide[:, :occ] + wide[:, occ:] + dot(low, both[span, :occ])
    coef_high, coef_low = coefficients(inter, count)
    coef = jnp.concatenate([coef_high, coef_low], axis=0)
    for shift in range(groups):
        span = columns(shift)
        wide = dot(coef, high_ref[:, :, span].reshape(rows, width))
        narrow = dot(coef_high, low_ref[:, :, span].reshape(rows, width))
        total[:, span] += wide[:occ] + wide[occ:] + narrow


def first_part(pieces, direction, before, offset, held):
    groups = len(pieces)
    count, occ, width = pieces[0].shape
    whole = groups * width
    step = max(s for s in (8, 4, 2, 1) if count % s == 0 and offset % s == 0)
    fixed = pl.BlockSpec((occ, whole), lambda s: (0, 0))
    in_specs = [pl.BlockSpec((step, occ, width), lambda s: (s, 0, 0))] * groups + [fixed]
    args = [*pieces, direction]
    aliases = {}
    first = before is None
    if first:
        shape = jax.ShapeDtypeStruct((held, occ, whole), BF16)
    else:
        total, high, low = before
        in_specs += [fixed, pl.BlockSpec(memory_space=pl.ANY), pl.BlockSpec(memory_space=pl.ANY)]
        args += [total, high, low]
        aliases = {groups + 2: 0, groups + 3: 1, groups + 1: 2}
        shape = jax.ShapeDtypeStruct(high.shape, BF16)
    start = offset // step
    store = pl.BlockSpec((step, occ, whole), lambda s: (start + s, 0, 0))
    high, low, total = pl.pallas_call(
        functools.partial(first_kernel, first, groups),
        grid=(count // step,),
        in_specs=in_specs,
        out_specs=[store, store, fixed],
        out_shape=[shape, shape, jax.ShapeDtypeStruct((occ, whole), F32)],
        scratch_shapes=[pltpu.VMEM((whole, 2 * occ), BF16)],
        input_output_aliases=aliases,
        compiler_params=pltpu.CompilerParams(vmem_limit_bytes=48 * 1024 * 1024),
    )(*args)
    return total, high, low


def advance(summed, gap, direction, residual, iterate):
    image = gap * direction + summed
    norm = jnp.sum(residual * residual)
    step = norm / jnp.sum(direction * image)
    return iterate + step * direction, residual - step * image, norm


def later_kernel(high_ref, low_ref, summed, gap, direction, residual, iterate,
                 total, new_direction, new_residual, new_iterate, both):
    count, occ, whole = high_ref.shape

    @pl.when(pl.program_id(0) == 0)
    def _():
        point, left, norm = advance(summed[...], gap[...], direction[...], residual[...], iterate[...])
        along = left + (jnp.sum(left * left) / norm) * direction[...]
        new_iterate[...] = point
        new_residual[...] = left
        new_direction[...] = along
        load_direction(along, both)
        total[...] = jnp.zeros_like(total)

    spans = [slice(n * (count // 2), (n + 1) * (count // 2)) for n in range(2)] if count > 1 else [slice(0, 1)]
    inters = []
    for span in spans:
        wide = dot(high_ref[span].reshape(-1, whole), both[...])
        narrow = dot(low_ref[span].reshape(-1, whole), both[:, :occ])
        inters.append(wide[:, :occ] + wide[:, occ:] + narrow)
    for span, inter in zip(spans, inters):
        coef_high, coef_low = coefficients(inter, span.stop - span.start)
        coef = jnp.concatenate([coef_high, coef_low], axis=0)
        wide = dot(coef, high_ref[span].reshape(-1, whole))
        narrow = dot(coef_high, low_ref[span].reshape(-1, whole))
        total[...] += wide[:occ] + wide[occ:] + narrow


def later_apply(high, low, *state):
    held, occ, whole = high.shape
    step = max(s for s in (16, 8, 4, 2, 1) if held % s == 0)
    fixed = pl.BlockSpec((occ, whole), lambda s: (0, 0))
    block = pl.BlockSpec((step, occ, whole), lambda s: (s, 0, 0))
    return pl.pallas_call(
        later_kernel,
        grid=(held // step,),
        in_specs=[block, block] + [fixed] * 5,
        out_specs=[fixed] * 4,
        out_shape=[jax.ShapeDtypeStruct((occ, whole), F32)] * 4,
        scratch_shapes=[pltpu.VMEM((whole, 2 * occ), BF16)],
        compiler_params=pltpu.CompilerParams(vmem_limit_bytes=48 * 1024 * 1024),
    )(high, low, *state)


def add_over(pieces, axes):
    return jnp.sum(lax.all_to_all(pieces, axes, split_axis=0, concat_axis=0, tiled=True), axis=0)


def add_up(total, mine, groups):
    occ, whole = total.shape
    rows = add_over(total.reshape(occ // mine, mine, whole), "aux")
    rows = add_over(jnp.broadcast_to(rows[None], (groups, mine, whole)), "vir")
    return lax.all_gather(rows, "aux", axis=0, tiled=True)


def on_device(groups, integrals, occupied_energy, virtual_energy, right_side):
    aux_rows, occ, width = integrals.shape
    whole = groups * width
    unit = aux_rows // groups // sum(PARTS)
    mine = occupied_energy.shape[0]
    me = lax.axis_index("vir")

    def start_and_gaps(earlier):
        first, occupied, _ = lax.optimization_barrier((right_side, occupied_energy, earlier))
        rows = jnp.concatenate(
            [first.T, jnp.broadcast_to(occupied[:, None], (mine, 128))], axis=1
        )
        rows = lax.all_gather(rows, "aux", axis=0, tiled=True)
        return jnp.stack([rows[:, :width], virtual_energy[None, :] - rows[:, width : width + 1]])

    def shifted(array, shift):
        return lax.ppermute(array, "vir", [(z, (z + shift) % groups) for z in range(groups)])

    def by_source(pieces):
        turned = pieces[:0:-1] + pieces[:1]
        twice = jnp.concatenate(turned + turned[:-1], axis=1)
        return lax.dynamic_slice(twice, (0, (groups - 1 - me) * width), (occ, whole))

    received = []
    held = start = None
    low_row = offset = applied = 0

    def apply_part():
        nonlocal held, offset, applied
        held = first_part(received[applied], start, held, offset, aux_rows // groups)
        offset += PARTS[applied] * unit
        applied += 1

    for k, share in enumerate(PARTS):
        count = share * unit
        if k == CARRIER:
            integrals, _ = lax.optimization_barrier((integrals, received[0][1]))
        blocks = [
            lax.dynamic_slice_in_dim(
                integrals, low_row + lax.rem(me + shift, groups) * count, count, axis=0
            )
            for shift in range(groups)
        ]
        low_row += groups * count
        if k == 0:
            blocks, integrals = lax.optimization_barrier((blocks, integrals))
        sent = blocks[1:]
        if k == CARRIER:
            carried = start_and_gaps(received[0][1])
            sent = [jnp.concatenate([block, carried], axis=0) for block in sent]
        if k >= DEPTH:
            while start is not None and k - DEPTH >= CARRIER and applied <= k - DEPTH:
                apply_part()
            if held is None:
                sent, _ = lax.optimization_barrier((sent, received[k - DEPTH]))
            else:
                total, high, low = held
                sent, total, start, gap = lax.optimization_barrier((sent, total, start, gap))
                held = total, high, low
        arrived = [shifted(block, n) for n, block in enumerate(sent, 1)]
        received.append(blocks[:1] + arrived)
        if k == CARRIER:
            own_and_others = [carried] + [piece[count:] for piece in arrived]
            start, gap = (by_source([piece[n] for piece in own_and_others]) for n in range(2))
    while applied < len(PARTS):
        apply_part()
    total, high, low = held

    direction = residual = start
    iterate = jnp.zeros_like(start)
    for _ in range(ITERS - 1):
        summed = add_up(total, mine, groups)
        total, direction, residual, iterate = later_apply(
            high, low, summed, gap, direction, residual, iterate
        )

    def own(array):
        return lax.dynamic_slice(array, (lax.axis_index("aux") * mine, me * width), (mine, width))

    product = jnp.full((occ // mine, groups, 1, width), jnp.sum(direction * total), F32)
    blocks = jnp.swapaxes(total.reshape(occ // mine, mine, groups, width), 1, 2)
    blocks = jnp.concatenate([blocks, product], axis=2).reshape(-1, mine + 1, width)
    block = add_over(blocks, ("aux", "vir"))
    product = block[mine, 0] + jnp.sum(gap * direction * direction)
    size = jnp.sum(residual * residual) / product
    image = own(gap) * own(direction) + block[:mine]
    iterate = own(iterate) + size * own(direction)
    residual = own(residual) - size * image
    return iterate.T, residual.T


def solution(mesh):
    in_specs = (P("aux", None, "vir"), P("aux"), P("vir"), P("vir", "aux"))
    out_specs = (P("vir", "aux"), P("vir", "aux"))
    return jax.shard_map(
        functools.partial(on_device, mesh.shape["vir"]),
        mesh=mesh,
        in_specs=in_specs,
        out_specs=out_specs,
        check_vma=False,
    )
```

```python
import functools

import jax
import jax.numpy as jnp
from jax import lax
from jax.experimental import pallas as pl
from jax.experimental.pallas import tpu as pltpu
from jax.sharding import PartitionSpec as P

ITERS = 3
PARTS = (1, 2, 2, 3, 3, 2, 2, 1)
DEPTH = 3
BF16 = jnp.bfloat16
F32 = jnp.float32


def halves(value):
    high = value.astype(BF16)
    return high, (value - high.astype(F32)).astype(BF16)


def load_direction(direction, both):
    occ = direction.shape[0]
    high, low = halves(direction.T)
    both[:, :occ] = high
    both[:, occ:] = low


def coefficients(inter, count):
    occ = inter.shape[1]
    rows = lax.broadcasted_iota(jnp.int32, (occ, occ), 0)
    cols = lax.broadcasted_iota(jnp.int32, (occ, occ), 1)
    diagonal = rows == cols
    highs, lows = [], []
    for p in range(count):
        block = inter[p * occ : (p + 1) * occ]
        trace = jnp.sum(jnp.where(diagonal, block, 0.0))
        high, low = halves(jnp.where(diagonal, 4.0 * trace, 0.0) - block)
        highs.append(high)
        lows.append(low)
    return jnp.concatenate(highs, axis=1), jnp.concatenate(lows, axis=1)


def dot(a, b):
    return jnp.dot(a, b, preferred_element_type=F32)


def first_kernel(first, groups, *refs):
    pieces, direction, rest = refs[:groups], refs[groups], refs[groups + 1 :]
    if first:
        high_ref, low_ref, total, both = rest
    else:
        before, _, _, high_ref, low_ref, total, both = rest
    count, occ, width = pieces[0].shape
    rows = count * occ
    me = lax.axis_index("vir")

    def columns(shift):
        source = lax.rem(me - shift + groups, groups)
        return pl.ds(pl.multiple_of(source * width, width), width)

    @pl.when(pl.program_id(0) == 0)
    def _():
        load_direction(direction[...], both)
        total[...] = jnp.zeros_like(total) if first else before[...]

    inter = jnp.zeros((rows, occ), F32)
    for shift in range(groups):
        span = columns(shift)
        high, low = halves(pieces[shift][...].reshape(rows, width))
        high_ref[:, :, span] = high.reshape(count, occ, width)
        low_ref[:, :, span] = low.reshape(count, occ, width)
        wide = dot(high, both[span, :])
        inter += wide[:, :occ] + wide[:, occ:] + dot(low, both[span, :occ])
    coef_high, coef_low = coefficients(inter, count)
    coef = jnp.concatenate([coef_high, coef_low], axis=0)
    for shift in range(groups):
        span = columns(shift)
        wide = dot(coef, high_ref[:, :, span].reshape(rows, width))
        narrow = dot(coef_high, low_ref[:, :, span].reshape(rows, width))
        total[:, span] += wide[:occ] + wide[occ:] + narrow


def first_part(pieces, direction, before, offset, held):
    groups = len(pieces)
    count, occ, width = pieces[0].shape
    whole = groups * width
    step = max(s for s in (8, 4, 2, 1) if count % s == 0 and offset % s == 0)
    fixed = pl.BlockSpec((occ, whole), lambda s: (0, 0))
    in_specs = [pl.BlockSpec((step, occ, width), lambda s: (s, 0, 0))] * groups + [fixed]
    args = [*pieces, direction]
    aliases = {}
    first = before is None
    if first:
        shape = jax.ShapeDtypeStruct((held, occ, whole), BF16)
    else:
        total, high, low = before
        in_specs += [fixed, pl.BlockSpec(memory_space=pl.ANY), pl.BlockSpec(memory_space=pl.ANY)]
        args += [total, high, low]
        aliases = {groups + 2: 0, groups + 3: 1, groups + 1: 2}
        shape = jax.ShapeDtypeStruct(high.shape, BF16)
    start = offset // step
    store = pl.BlockSpec((step, occ, whole), lambda s: (start + s, 0, 0))
    high, low, total = pl.pallas_call(
        functools.partial(first_kernel, first, groups),
        grid=(count // step,),
        in_specs=in_specs,
        out_specs=[store, store, fixed],
        out_shape=[shape, shape, jax.ShapeDtypeStruct((occ, whole), F32)],
        scratch_shapes=[pltpu.VMEM((whole, 2 * occ), BF16)],
        input_output_aliases=aliases,
        compiler_params=pltpu.CompilerParams(vmem_limit_bytes=48 * 1024 * 1024),
    )(*args)
    return total, high, low


def advance(summed, gap, direction, residual, iterate):
    image = gap * direction + summed
    norm = jnp.sum(residual * residual)
    step = norm / jnp.sum(direction * image)
    return iterate + step * direction, residual - step * image, norm


def later_kernel(high_ref, low_ref, summed, gap, direction, residual, iterate,
                 total, new_direction, new_residual, new_iterate, both):
    count, occ, whole = high_ref.shape

    @pl.when(pl.program_id(0) == 0)
    def _():
        point, left, norm = advance(summed[...], gap[...], direction[...], residual[...], iterate[...])
        along = left + (jnp.sum(left * left) / norm) * direction[...]
        new_iterate[...] = point
        new_residual[...] = left
        new_direction[...] = along
        load_direction(along, both)
        total[...] = jnp.zeros_like(total)

    spans = [slice(n * (count // 2), (n + 1) * (count // 2)) for n in range(2)] if count > 1 else [slice(0, 1)]
    inters = []
    for span in spans:
        wide = dot(high_ref[span].reshape(-1, whole), both[...])
        narrow = dot(low_ref[span].reshape(-1, whole), both[:, :occ])
        inters.append(wide[:, :occ] + wide[:, occ:] + narrow)
    for span, inter in zip(spans, inters):
        coef_high, coef_low = coefficients(inter, span.stop - span.start)
        coef = jnp.concatenate([coef_high, coef_low], axis=0)
        wide = dot(coef, high_ref[span].reshape(-1, whole))
        narrow = dot(coef_high, low_ref[span].reshape(-1, whole))
        total[...] += wide[:occ] + wide[occ:] + narrow


def later_apply(high, low, *state):
    held, occ, whole = high.shape
    step = max(s for s in (16, 8, 4, 2, 1) if held % s == 0)
    fixed = pl.BlockSpec((occ, whole), lambda s: (0, 0))
    block = pl.BlockSpec((step, occ, whole), lambda s: (s, 0, 0))
    return pl.pallas_call(
        later_kernel,
        grid=(held // step,),
        in_specs=[block, block] + [fixed] * 5,
        out_specs=[fixed] * 4,
        out_shape=[jax.ShapeDtypeStruct((occ, whole), F32)] * 4,
        scratch_shapes=[pltpu.VMEM((whole, 2 * occ), BF16)],
        compiler_params=pltpu.CompilerParams(vmem_limit_bytes=48 * 1024 * 1024),
    )(high, low, *state)


def add_over(pieces, axes):
    return jnp.sum(lax.all_to_all(pieces, axes, split_axis=0, concat_axis=0, tiled=True), axis=0)


def add_up(total, mine, groups):
    occ, whole = total.shape
    rows = add_over(total.reshape(occ // mine, mine, whole), "aux")
    rows = add_over(jnp.broadcast_to(rows[None], (groups, mine, whole)), "vir")
    return lax.all_gather(rows, "aux", axis=0, tiled=True)


def on_device(groups, integrals, occupied_energy, virtual_energy, right_side):
    aux_rows, occ, width = integrals.shape
    whole = groups * width
    unit = aux_rows // groups // sum(PARTS)
    mine = occupied_energy.shape[0]
    me = lax.axis_index("vir")

    def start_and_gaps(known):
        rows = jnp.concatenate(
            [known[:mine], jnp.broadcast_to(occupied_energy[:, None], (mine, 128))], axis=1
        )
        rows = lax.all_gather(rows, "aux", axis=0, tiled=True)
        return rows[:, :whole], known[mine:] - rows[:, whole : whole + 1]

    def shifted(array, shift):
        return lax.ppermute(array, "vir", [(z, (z + shift) % groups) for z in range(groups)])

    def by_source(pieces):
        turned = pieces[:0:-1] + pieces[:1]
        twice = jnp.concatenate(turned + turned[:-1], axis=1)
        return lax.dynamic_slice(twice, (0, (groups - 1 - me) * width), (mine + 1, whole))

    rows = jnp.concatenate([right_side.T, virtual_energy[None, :]], axis=0)
    known = by_source([rows] + [shifted(rows, n) for n in range(1, groups)])

    received = []
    held = start = None
    low_row = offset = applied = 0

    def apply_part():
        nonlocal held, offset, applied
        held = first_part(received[applied], start, held, offset, aux_rows // groups)
        offset += PARTS[applied] * unit
        applied += 1

    for k, share in enumerate(PARTS):
        count = share * unit
        if k == 2:
            integrals, _ = lax.optimization_barrier((integrals, received[0][1]))
        blocks = [
            lax.dynamic_slice_in_dim(
                integrals, low_row + lax.rem(me + shift, groups) * count, count, axis=0
            )
            for shift in range(groups)
        ]
        low_row += groups * count
        if k == 0:
            blocks, integrals = lax.optimization_barrier((blocks, integrals))
        sent = blocks[1:]
        if k == 2:
            sent, known = lax.optimization_barrier((sent, known))
        if k == DEPTH:
            start, gap = start_and_gaps(known)
        if k >= DEPTH:
            apply_part()
            total, high, low = held
            sent, total, start, gap = lax.optimization_barrier((sent, total, start, gap))
            held = total, high, low
        received.append(blocks[:1] + [shifted(block, n) for n, block in enumerate(sent, 1)])
    while applied < len(PARTS):
        apply_part()
    total, high, low = held

    direction = residual = start
    iterate = jnp.zeros_like(start)
    for _ in range(ITERS - 1):
        summed = add_up(total, mine, groups)
        total, direction, residual, iterate = later_apply(
            high, low, summed, gap, direction, residual, iterate
        )

    def own(array):
        return lax.dynamic_slice(array, (lax.axis_index("aux") * mine, me * width), (mine, width))

    product = jnp.full((occ // mine, groups, 1, width), jnp.sum(direction * total), F32)
    blocks = jnp.swapaxes(total.reshape(occ // mine, mine, groups, width), 1, 2)
    blocks = jnp.concatenate([blocks, product], axis=2).reshape(-1, mine + 1, width)
    block = add_over(blocks, ("aux", "vir"))
    product = block[mine, 0] + jnp.sum(gap * direction * direction)
    size = jnp.sum(residual * residual) / product
    image = own(gap) * own(direction) + block[:mine]
    iterate = own(iterate) + size * own(direction)
    residual = own(residual) - size * image
    return iterate.T, residual.T


def solution(mesh):
    in_specs = (P("aux", None, "vir"), P("aux"), P("vir"), P("vir", "aux"))
    out_specs = (P("vir", "aux"), P("vir", "aux"))
    return jax.shard_map(
        functools.partial(on_device, mesh.shape["vir"]),
        mesh=mesh,
        in_specs=in_specs,
        out_specs=out_specs,
        check_vma=False,
    )
```
